32 devices in a mesh: section: 4 (over z), expert: 8 (over y, x, core).
Axes of the slice: x: 2, y: 2, z: 4, core: 2. Of those that a mesh axis runs over, the one named last changes fastest.
Arguments:
- d_output: bfloat16 [4096, 4096], P(('section', 'expert')), may hold values from -3 to 3
- gate_values: bfloat16 [4096, 8], P(('section', 'expert')), may hold values from 0.049804688 to 0.5
- routes: int32 [4096, 8], P(('section', 'expert')), may hold values from 0 to 15, all different within a row; in each aligned block of 128 rows (0 to 127, 128 to 255, ...) at most 72 rows name the same one
- hidden_saved: bfloat16 [4, 16, 8, 72, 768], P('section', 'expert'), may hold values from -3 to 3
- w_down: bfloat16 [16, 768, 4096], P('expert'), may hold values from -0.21875 to 0.21875
Outputs:
- d_hidden: bfloat16 [4, 16, 8, 72, 768], P('section', 'expert')
- d_weight: bfloat16 [16, 768, 4096], P('expert', 'section')
- d_gate: float32 [4096, 8], P(('section', 'expert'))
The draws below stay inside these ranges and needn't reach their ends.
Inputs may be any that keep to these rules, and one draw needn't show every extreme that they name: `routes`: each row names 8 different experts. Within the rows of one device (128 tokens) no expert is named by more than 72 rows, a bound that some block reaches.
All inputs are finite; a program needn't handle non-finite values.
Results may differ from the reference program's by a relative error of at most 0.017.
Values may be sent and summed in bfloat16 or wider, within the bound.
A program may use at most 192 MiB of HBM per device.

```python
import math
import jax
import jax.numpy as jnp
import numpy as np
from jax import lax

D = 4096
FF = 768
TOPK = 8
TOK_DEV = 128
EXPERTS = 16
CAP = 72
SLICES = 4
TOKENS = 4096
N_EXPERT = 8


def block_levels(key, shape, pieces, least, largest):
    factor_of, own = 1.0, jax.random.fold_in(key, 6)
    for axis_at, blocks in pieces:
        heights = jnp.exp(jax.random.uniform(jax.random.fold_in(own, axis_at), (blocks,), jnp.float32, least / len(pieces), largest / len(pieces)))
        factor_of = factor_of * jnp.repeat(heights, shape[axis_at] // blocks).reshape([-1 if axis == axis_at else 1 for axis in range(len(shape))])
    return factor_of


def assign_block(own_key, own, number, rows, amount, top, limit, skew):
    order = jax.random.permutation(own_key, amount)
    heavy_load, ordinary = portions_of(amount, rows * top, limit, skew, True), portions_of(amount, rows * top, limit, skew, False)
    places = jnp.arange(amount)

    def named(tallies, offset_by):
        used = int((tallies > 0).sum())
        fixed = max(1, used // 4)
        shifted = fixed + (places - fixed + offset_by * (used - fixed)) % max(1, amount - fixed)
        return jnp.zeros((amount,), jnp.int32).at[order[jnp.where(places < fixed, places, shifted)]].set(jnp.asarray(tallies, jnp.int32))

    tallies = jnp.where(number % 4 == 0, named(heavy_load, number // 4), named(ordinary, number - number // 4 - 1))
    mixed = jax.random.permutation(jax.random.fold_in(own, 3), amount)
    donor, taker = mixed[0:amount // 2 * 2:2], mixed[1:amount // 2 * 2:2]
    margin = jnp.minimum(tallies[donor] - 1, limit - tallies[taker]) // 2
    margin = jnp.where((donor == order[0]) | (taker == order[0]) | (tallies[taker] == 0), 0, jnp.maximum(margin, 0))
    shifted = jax.random.randint(jax.random.fold_in(own, 4), (amount // 2,), 0, 1 << 20) % (margin + 1)
    tallies = tallies.at[donor].add(-shifted).at[taker].add(shifted)
    labels = jnp.searchsorted(jnp.cumsum(tallies), jnp.arange(rows * top), side="right").astype(jnp.int32)
    listing = labels.reshape(top, rows).T
    listing = listing[jax.random.permutation(jax.random.fold_in(own, 1), rows)]
    offset_by = jax.random.randint(jax.random.fold_in(own, 2), (rows, 1), 0, top)
    return jnp.take_along_axis(listing, (jnp.arange(top)[None, :] + offset_by) % top, axis=1)


def portions_of(count, total, bound, lean, full):
    portions = [(1 << 20) // math.isqrt(grade ** lean) + 1 for grade in range(1, count + 1)]
    largest = bound if full else min(bound, max(-(-total // count), total * portions[0] // sum(portions)))
    least = 1 if total - largest >= count - 1 else 0
    given, rest = [largest] + [least] * (count - 1), total - largest - least * (count - 1)
    while rest > 0:
        candidates = [i for i in range(1, count) if given[i] < largest] or [i for i in range(1, count) if given[i] < bound]
        pool, budget = sum([portions[i] for i in candidates]), rest
        for i in candidates:
            addition = min(bound - given[i], max(1, budget * portions[i] // pool), rest)
            given[i] = given[i] + addition
            rest = rest - addition
    return np.array(given)


def normal_values(stream_key, shape, spread, most, cuts=(), held_as=jnp.bfloat16):
    gain = block_levels(stream_key, shape, cuts, -0.22, 0.18) if cuts else 1.0
    drawn = jax.random.normal(stream_key, shape, jnp.float32) * spread * gain
    return jnp.minimum(jnp.maximum(drawn, -most), most).astype(held_as)


def setup_inputs(seed: int = 0) -> dict:
    splits = jax.random.split(jax.random.key(seed), 6)
    d_output = normal_values(splits[0], (TOKENS, D), 0.5, 3.0, ((0, 32),))
    gate_values = jnp.clip(jnp.exp(math.log(0.5) - 2.306499 * jax.random.uniform(splits[1], (TOKENS, TOPK), jnp.float32) ** block_levels(splits[1], (TOKENS, TOPK), ((0, 32),), -0.2, 0.2)), 0.049804688, 0.5).astype(jnp.bfloat16)
    routes_keys = jax.random.split(jax.random.fold_in(splits[2], 1), TOKENS // TOK_DEV)
    routes_turns = jax.random.permutation(jax.random.fold_in(splits[2], 3), TOKENS // TOK_DEV)
    routes = jax.vmap(lambda own, number: assign_block(jax.random.fold_in(splits[2], 2), own, number, TOK_DEV, EXPERTS, TOPK, CAP, 2))(routes_keys, routes_turns).reshape((TOKENS, TOPK))
    hidden_saved = normal_values(splits[3], (SLICES, EXPERTS, N_EXPERT, CAP, FF), 0.5, 3.0, ((0, 4), (1, 8)))
    w_down = normal_values(splits[4], (EXPERTS, FF, D), FF ** -0.5, 0.21875, ((0, 8),))
    return {"d_output": d_output, "gate_values": gate_values, "routes": routes, "hidden_saved": hidden_saved, "w_down": w_down}


def slot_ranks(route_block, expert_count):
    one_hot = (route_block[..., None] == jnp.arange(expert_count, dtype=jnp.int32)).astype(jnp.int32)
    earlier = jnp.cumsum(one_hot, axis=1) - one_hot
    return jnp.sum(earlier * one_hot, axis=2)


def reference(d_output, gate_values, routes, hidden_saved, w_down):
    weight_wide = w_down.astype(jnp.float32)
    pair_count = TOK_DEV * TOPK
    dy_all = d_output.reshape(SLICES, N_EXPERT * TOK_DEV, D)
    gate_all = gate_values.reshape(SLICES, N_EXPERT * TOK_DEV, TOPK)
    route_all = routes.reshape(SLICES, N_EXPERT * TOK_DEV, TOPK)

    def per_slice(weight_total, inputs):
        dy_slice, gate_slice, route_slice, hidden_slice = inputs
        route_block = route_slice.reshape(N_EXPERT, pair_count).astype(jnp.int32)
        slot_rank = slot_ranks(route_block, EXPERTS)
        source_dev = jnp.arange(N_EXPERT, dtype=jnp.int32)[:, None]
        slot_index = (route_block * (N_EXPERT * CAP) + source_dev * CAP + slot_rank).reshape(-1).astype(jnp.int32)
        gated = (gate_slice.astype(jnp.float32)[:, :, None] * dy_slice.astype(jnp.float32)[:, None, :]).astype(jnp.bfloat16)
        dispatched = jnp.zeros((EXPERTS * N_EXPERT * CAP, D), jnp.bfloat16).at[slot_index].set(gated.reshape(-1, D))
        dispatched = dispatched.reshape(EXPERTS, N_EXPERT * CAP, D).astype(jnp.float32)
        hidden_wide = hidden_slice.reshape(EXPERTS, N_EXPERT * CAP, FF).astype(jnp.float32)
        d_hidden_slice = jnp.einsum("erd,efd->erf", dispatched, weight_wide).astype(jnp.bfloat16)
        partial_value = jnp.einsum("erf,erd->efd", hidden_wide, dispatched).astype(jnp.bfloat16)
        partial_value = lax.optimization_barrier(partial_value).astype(jnp.float32)
        expert_rows = jnp.einsum("erf,efd->erd", hidden_wide, weight_wide).astype(jnp.bfloat16)
        picked = expert_rows.reshape(-1, D)[slot_index].reshape(N_EXPERT * TOK_DEV, TOPK, D)
        d_gate_slice = jnp.sum(dy_slice.astype(jnp.float32)[:, None, :] * picked.astype(jnp.float32), axis=2)
        return weight_total + partial_value, (d_hidden_slice.reshape(EXPERTS, N_EXPERT, CAP, FF), d_gate_slice)

    start = jnp.zeros((EXPERTS, FF, D), jnp.float32)
    weight_total, (d_hidden, d_gate) = lax.scan(per_slice, start, (dy_all, gate_all, route_all, hidden_saved))
    return d_hidden, weight_total.astype(jnp.bfloat16), d_gate.reshape(TOKENS, TOPK)
```

```python
import jax
import jax.numpy as jnp
from jax import lax
from jax.sharding import PartitionSpec as P


def shards(d_output, gate_values, routes, hidden_saved, w_down):
    held, hidden_width, width = w_down.shape
    tok = d_output.shape[0]
    sources, capacity = hidden_saved.shape[2], hidden_saved.shape[3]
    sections = lax.axis_size("section")
    expert_count = held * sources
    me = lax.axis_index("expert")
    f32, bf16 = jnp.float32, jnp.bfloat16

    match = routes[:, :, None] == jnp.arange(expert_count, dtype=jnp.int32)
    chosen = jnp.any(match, axis=1).astype(jnp.int32)
    rank = jnp.where(chosen > 0, jnp.cumsum(chosen, axis=0) - chosen, -1)
    gate = jnp.sum(jnp.where(match, gate_values[:, :, None].astype(f32), 0.0), axis=1)
    table = jnp.stack([rank.T.astype(bf16), gate.T.astype(bf16)])
    table = lax.all_gather(table, ("section", "expert"))
    mine = lax.dynamic_slice_in_dim(table, me * held, held, axis=2)
    mine = mine.reshape(sections, sources, 2, held, tok)

    by_section = lax.all_gather(d_output, "section")
    dy = lax.all_gather(by_section, "expert", axis=1)

    blocks = hidden_saved[0].reshape(held, sources, capacity, sections, -1)
    blocks = jnp.transpose(blocks, (3, 0, 1, 2, 4))
    parts = lax.all_to_all(blocks, "section", split_axis=0, concat_axis=0, tiled=True)

    slots = jnp.arange(capacity, dtype=jnp.int32)
    slot_of = mine[:, :, 0].astype(jnp.int32)
    pick = (slot_of[..., None] == slots) * mine[:, :, 1].astype(f32)[..., None]
    scattered = jnp.einsum(
        "sjetc,sejcf->sjtef", pick.astype(bf16), parts, preferred_element_type=f32
    ).astype(bf16)
    d_weight = jnp.einsum("sjtef,sjtd->efd", scattered, dy, preferred_element_type=f32).astype(
        bf16
    )

    own = lax.axis_index("section")
    dy_own = lax.dynamic_index_in_dim(dy, own, 0, keepdims=False)
    rank_own = lax.dynamic_index_in_dim(slot_of, own, 0, keepdims=False)
    gate_own = lax.dynamic_index_in_dim(mine[:, :, 1], own, 0, keepdims=False)
    select = rank_own[:, :, None, :] == slots[:, None]
    gate_slot = jnp.sum(jnp.where(select, gate_own.astype(f32)[:, :, None, :], 0.0), axis=3)
    rows = jnp.einsum(
        "ject,jtd->ejcd", select.astype(bf16), dy_own, preferred_element_type=f32
    ).astype(bf16)
    plain = jnp.einsum("ejcd,efd->ejcf", rows, w_down, preferred_element_type=f32)
    gate_ejc = jnp.transpose(gate_slot, (1, 0, 2))
    d_hidden = (plain * gate_ejc[..., None]).astype(bf16)[None]
    value = jnp.sum(plain * hidden_saved[0].astype(f32), axis=3)
    token_value = jnp.sum(
        jnp.where(select, jnp.transpose(value, (1, 0, 2))[..., None], 0.0), axis=2
    )
    back = lax.all_to_all(token_value, "expert", split_axis=0, concat_axis=0, tiled=True)
    back = back.reshape(expert_count, tok)
    d_gate = jnp.sum(jnp.where(match, back.T[:, None, :], 0.0), axis=2)
    return d_hidden, d_weight, d_gate


def solution(mesh):
    placed = (
        P(("section", "expert"), None),
        P(("section", "expert"), None),
        P(("section", "expert"), None),
        P("section", "expert", None, None, None),
        P("expert", None, None),
    )
    return jax.shard_map(
        shards,
        mesh=mesh,
        in_specs=placed,
        out_specs=(
            P("section", "expert", None, None, None),
            P("expert", "section", None),
            P(("section", "expert"), None),
        ),
        check_vma=False,
    )
```

```python
import functools

import jax
import jax.numpy as jnp
from jax import lax
from jax.experimental import pallas as pl
from jax.experimental.pallas import tpu as pltpu
from jax.sharding import PartitionSpec as P

MESH = pl.DeviceIdType.MESH
TILE = 512


def flipped(index, bits):
    for bit in bits:
        index = index + bit * (1 - 2 * ((index // bit) % 2))
    return index


def dot(a, b, dims):
    return lax.dot_general(a, b, (dims, ((), ())), preferred_element_type=jnp.float32)


def body(sections, sources, dy_ref, tab_ref, hid_ref, blocks_ref, w_ref,
         all_ref, dw_ref, dh_ref, back_ref,
         tabs, parts, dy_vm, w_vm, acc, scattered, picked, rows_vm, plain, token_vm, back_vm,
         local_sem, z_send, z_recv, h_send, h_recv, e_send, e_recv, b_send, b_recv):
    f32, bf16 = jnp.float32, jnp.bfloat16
    z, j = lax.axis_index("section"), lax.axis_index("expert")
    tok, width = dy_ref.shape
    held, slot_rows, hidden_width = hid_ref.shape
    pairs = sources // 2
    pair_rows = slot_rows // pairs
    capacity = pair_rows // 2
    part_width = blocks_ref.shape[2] // held
    expert_count = tab_ref.shape[0] // 2
    half_rows = tok // 2
    bits = [1 << b for b in range(sources.bit_length() - 1)]
    orders = (bits[1:] + bits[:1], bits[1:][::-1] + bits[:1])
    steps = [0]
    for d in range(1, sections):
        steps.append((d + 1) // 2 if d % 2 else sections - d // 2)

    def section_at(i):
        return (z + sections - steps[i]) % sections

    tabs[z, j] = tab_ref[...]
    barrier = pltpu.get_barrier_semaphore()
    for d in range(1, sections):
        pl.semaphore_signal(barrier, inc=1, device_id=((z + d) % sections, j), device_id_type=MESH)
    for r in range(1, sources):
        pl.semaphore_signal(barrier, inc=1, device_id=(z, (j + r) % sources), device_id_type=MESH)
    pl.semaphore_wait(barrier, sections + sources - 2)

    own_dy = pltpu.make_async_copy(dy_ref, all_ref.at[z, pl.ds(pl.multiple_of(j * tok, tok), tok)], local_sem.at[0])
    own_hid = pltpu.make_async_copy(blocks_ref.at[z], parts.at[z], local_sem.at[1])
    get_w = pltpu.make_async_copy(w_ref, w_vm, local_sem.at[2])

    def remote(source, target, send, recv, to):
        return pltpu.make_async_remote_copy(
            source, target, send, recv, device_id=to, device_id_type=MESH)

    def block_at(s, block, start, count):
        return all_ref.at[s, pl.ds(pl.multiple_of(block * tok + start, 16), count)]

    z_copies, h_copies = [None], [None]
    for i in range(1, sections):
        to = (z + steps[i]) % sections
        z_copies.append([
            remote(dy_ref, block_at(z, j, 0, tok), z_send.at[i, 0], z_recv.at[i, 0], (to, j)),
            remote(tabs.at[z, j], tabs.at[z, j], z_send.at[i, 1], z_recv.at[i, 1], (to, j)),
        ])
        h_copies.append(remote(blocks_ref.at[to], parts.at[z], h_send.at[i], h_recv.at[i], (to, j)))

    stage = {}

    def begin(i, k):
        s = section_at(i)
        stage[i, k] = []
        for part in range(3):
            order = orders[part % 2]
            have = [[]]
            for bit in order[:k]:
                have = have + [r + [bit] for r in have]
            to = (z, flipped(j, [order[k]]))
            for r in have:
                block = flipped(j, r)
                slot = sum(r) + order[k]
                sems = e_send.at[i, part, slot], e_recv.at[i, part, slot]
                if part == 2:
                    copy = remote(tabs.at[s, block], tabs.at[s, block], *sems, to)
                else:
                    target = block_at(s, block, part * half_rows, half_rows)
                    source = target
                    if i == 0 and not r:
                        source = dy_ref.at[pl.ds(part * half_rows, half_rows)]
                    copy = remote(source, target, *sems, to)
                copy.start()
                stage[i, k].append(copy)

    def arrive(i, k):
        for copy in stage[i, k]:
            copy.wait_recv()

    last = len(bits) - 1

    def fetch(i):
        load = pltpu.make_async_copy(all_ref.at[section_at(i)], dy_vm, local_sem.at[3])
        load.start()
        load.wait()

    def row_of(i, p, row):
        s = section_at(i)
        return jnp.concatenate(
            [tabs[s, 2 * p, pl.ds(row, 1), :], tabs[s, 2 * p + 1, pl.ds(row, 1), :]], axis=1)

    def rank_row(i, p, e):
        rank = row_of(i, p, j * held + e)
        lane = lax.broadcasted_iota(jnp.int32, rank.shape, 1)
        return jnp.where(rank < 0, -1.0, rank + jnp.where(lane < tok, 0.0, float(capacity)))

    def gate_row(i, p, e):
        return row_of(i, p, expert_count + j * held + e)

    def chosen(i, p, e):
        place = lax.broadcasted_iota(jnp.int32, (pair_rows, 2 * tok), 0).astype(f32)
        return place == rank_row(i, p, e)

    def weight_part(i):
        s = section_at(i)
        for p in range(pairs):
            hid = parts[s, p * pair_rows:(p + 1) * pair_rows, :]
            for e in range(held):
                gates = jnp.where(chosen(i, p, e), gate_row(i, p, e), 0.0).astype(bf16)
                moved = dot(hid, gates, ((0,), (0,)))
                scattered[e * part_width:(e + 1) * part_width, p * 2 * tok:(p + 1) * 2 * tok] = (
                    moved[e * part_width:(e + 1) * part_width].astype(bf16))

        def tile(t, _):
            cols = pl.ds(pl.multiple_of(t * TILE, TILE), TILE)
            value = dot(scattered[...], dy_vm[:, cols], ((1,), (0,)))
            if i > 0:
                value = value + acc[:, cols]
            if i == sections - 1:
                dw_ref[:, cols] = value.astype(bf16)
            else:
                acc[:, cols] = value
            return 0

        lax.fori_loop(0, width // TILE, tile, 0)

    def hidden_part():
        for e in range(held):
            for p in range(pairs):
                picked[e, p] = jnp.where(chosen(0, p, e), 1.0, 0.0).astype(bf16)
            plain[e] = jnp.zeros(plain.shape[1:], f32)

        def tile(t, _):
            cols = pl.ds(pl.multiple_of(t * TILE, TILE), TILE)
            for e in range(held):
                for p in range(pairs):
                    rows_vm[p * pair_rows:(p + 1) * pair_rows, :] = dot(
                        picked[e, p], dy_vm[p * 2 * tok:(p + 1) * 2 * tok, cols], ((1,), (0,))
                    ).astype(bf16)
                plain[e] += dot(rows_vm[...], w_vm[e, :, cols], ((1,), (1,)))
            return 0

        lax.fori_loop(0, width // TILE, tile, 0)
        for e in range(held):
            for p in range(pairs):
                rows = slice(p * pair_rows, (p + 1) * pair_rows)
                here = chosen(0, p, e)
                gate = jnp.sum(jnp.where(here, gate_row(0, p, e), 0.0), axis=1, keepdims=True)
                value = plain[e, rows, :]
                dh_ref[e, rows, :] = (value * gate).astype(bf16)
                total = jnp.sum(value * hid_ref[e, rows, :].astype(f32), axis=1, keepdims=True)
                by_token = jnp.sum(jnp.where(here, total, 0.0), axis=0, keepdims=True)
                token_vm[2 * p, e:e + 1, :] = by_token[:, :tok]
                token_vm[2 * p + 1, e:e + 1, :] = by_token[:, tok:]

    b_copies = []
    for r in range(1, sources):
        to = (j + r) % sources
        b_copies.append(remote(token_vm.at[to], back_vm.at[j], b_send.at[r], b_recv.at[r], (z, to)))

    token_vm[...] = jnp.zeros(token_vm.shape, f32)
    begin(0, 0)
    own_dy.start()
    own_hid.start()
    get_w.start()
    if sections > 1:
        for copy in z_copies[1]:
            copy.start()
        h_copies[1].start()
    for i in range(sections):
        for k in range(1, last):
            arrive(i, k - 1)
            begin(i, k)
        if i + 1 < sections:
            for copy in z_copies[i + 1]:
                copy.wait()
            begin(i + 1, 0)
            if i + 2 < sections:
                for copy in z_copies[i + 2]:
                    copy.start()
            if i >= 2:
                h_copies[i].start()
            if i + 2 == sections and i + 1 >= 2:
                h_copies[i + 1].start()
        if i == 1:
            own_hid.wait()
            get_w.wait()
            hidden_part()
            for copy in b_copies:
                copy.start()
            back_vm[j] = token_vm[j]
            weight_part(0)
        elif i >= 2:
            fetch(i - 1)
            h_copies[i - 1].wait_recv()
            weight_part(i - 1)
        arrive(i, last - 1)
        begin(i, last)
        if i == 0:
            own_dy.wait()
            arrive(0, last)
            fetch(0)
        elif i + 1 < sections:
            arrive(i, last)
    final = sections - 1
    arrive(final, last)
    fetch(final)
    h_copies[final].wait_recv()
    weight_part(final)
    for copy in b_copies:
        copy.wait()
    back_ref[...] = back_vm[...]
    for copies in stage.values():
        for copy in copies:
            copy.wait_send()
    for copy in h_copies[1:]:
        copy.wait_send()


def fused(dy, table, hid, blocks, w, sections, sources):
    tok, width = dy.shape
    held, slot_rows, hidden_width = hid.shape
    part_rows = blocks.shape[2]
    pairs = sources // 2
    any_space, vmem = pl.BlockSpec(memory_space=pl.ANY), pl.BlockSpec(memory_space=pltpu.VMEM)
    dma = pltpu.SemaphoreType.DMA
    f32, bf16 = jnp.float32, jnp.bfloat16
    back = (sources, 8, tok)
    flops = 2 * width * (2 * slot_rows * held * hidden_width + sections * sources * tok * part_rows)
    return pl.pallas_call(
        functools.partial(body, sections, sources),
        out_shape=(
            jax.ShapeDtypeStruct((sections, sources * tok, width), bf16),
            jax.ShapeDtypeStruct((part_rows, width), bf16),
            jax.ShapeDtypeStruct(hid.shape, bf16),
            jax.ShapeDtypeStruct(back, f32),
        ),
        in_specs=[any_space, vmem, vmem, vmem, any_space],
        out_specs=(any_space, vmem, vmem, vmem),
        scratch_shapes=[
            pltpu.VMEM((sections, sources) + table.shape, f32),
            pltpu.VMEM(blocks.shape, bf16),
            pltpu.VMEM((sources * tok, width), bf16),
            pltpu.VMEM(w.shape, bf16),
            pltpu.VMEM((part_rows, width), f32),
            pltpu.VMEM((part_rows, sources * tok), bf16),
            pltpu.VMEM((held, pairs, slot_rows // pairs, 2 * tok), bf16),
            pltpu.VMEM((slot_rows, TILE), bf16),
            pltpu.VMEM(hid.shape, f32),
            pltpu.VMEM(back, f32),
            pltpu.VMEM(back, f32),
            dma((4,)), dma((sections, 2)), dma((sections, 2)), dma((sections,)), dma((sections,)),
            dma((sections, 3, sources)), dma((sections, 3, sources)), dma((sources,)), dma((sources,)),
        ],
        compiler_params=pltpu.CompilerParams(
            collective_id=0, has_side_effects=True, vmem_limit_bytes=58 * 1024 * 1024),
        cost_estimate=pl.CostEstimate(
            flops=flops, bytes_accessed=2 * sections * sources * tok * width * 2, transcendentals=0),
    )(dy, table, hid, blocks, w)


def shards(d_output, gate_values, routes, hidden_saved, w_down):
    held, hidden_width, width = w_down.shape
    tok = d_output.shape[0]
    sources, capacity = hidden_saved.shape[2], hidden_saved.shape[3]
    sections = lax.axis_size("section")
    expert_count = held * sources
    f32 = jnp.float32

    match = routes[:, :, None] == jnp.arange(expert_count, dtype=jnp.int32)
    chosen = jnp.any(match, axis=1).astype(jnp.int32)
    rank = jnp.where(chosen > 0, jnp.cumsum(chosen, axis=0) - chosen, -1)
    gate = jnp.sum(jnp.where(match, gate_values[:, :, None].astype(f32), 0.0), axis=1)
    table = jnp.concatenate([rank.T.astype(f32), gate.T], axis=0)

    hid = hidden_saved.reshape(held, sources * capacity, hidden_width)
    blocks = hid.reshape(held, sources * capacity, sections, hidden_width // sections)
    blocks = jnp.transpose(blocks, (2, 1, 0, 3)).reshape(sections, sources * capacity, -1)
    _, d_weight, d_hidden, back = fused(d_output, table, hid, blocks, w_down, sections, sources)
    back = back[:, :held].reshape(expert_count, tok)
    d_gate = jnp.sum(jnp.where(match, back.T[:, None, :], 0.0), axis=2)
    return (
        d_hidden.reshape(hidden_saved.shape),
        d_weight.reshape(held, hidden_width // sections, width),
        d_gate,
    )


def solution(mesh):
    placed = (
        P(("section", "expert"), None),
        P(("section", "expert"), None),
        P(("section", "expert"), None),
        P("section", "expert", None, None, None),
        P("expert", None, None),
    )
    return jax.shard_map(
        shards,
        mesh=mesh,
        in_specs=placed,
        out_specs=(
            P("section", "expert", None, None, None),
            P("expert", "section", None),
            P(("section", "expert"), None),
        ),
        check_vma=False,
    )
```

```python
import functools

import jax
import jax.numpy as jnp
from jax import lax
from jax.experimental import pallas as pl
from jax.experimental.pallas import tpu as pltpu
from jax.sharding import PartitionSpec as P

MESH = pl.DeviceIdType.MESH
TILE = 512


def flipped(index, bits):
    for bit in bits:
        index = index + bit * (1 - 2 * ((index // bit) % 2))
    return index


def dot(a, b, dims):
    return lax.dot_general(a, b, (dims, ((), ())), preferred_element_type=jnp.float32)


def body(sections, sources, dy_ref, route_ref, gates_ref, hid_ref, w_ref,
         all_ref, dw_ref, dh_ref, dg_ref,
         tabs, blocks_ref, parts, dy_vm, w_vm, acc, scattered, picked, rows_vm, plain, token_vm, back_vm,
         local_sem, z_send, z_recv, h_send, h_recv, e_send, e_recv, b_send, b_recv):
    f32, bf16 = jnp.float32, jnp.bfloat16
    z, j = lax.axis_index("section"), lax.axis_index("expert")
    tok, width = dy_ref.shape
    held, slot_rows, hidden_width = hid_ref.shape
    pairs = sources // 2
    pair_rows = slot_rows // pairs
    capacity = pair_rows // 2
    part_width = hidden_width // sections
    expert_count = held * sources
    half_rows = tok // 2
    bits = [1 << b for b in range(sources.bit_length() - 1)]
    orders = (bits[1:] + bits[:1], bits[1:][::-1] + bits[:1])
    steps = [0]
    for d in range(1, sections):
        steps.append((d + 1) // 2 if d % 2 else sections - d // 2)

    def section_at(i):
        return (z + sections - steps[i]) % sections

    expert_row = lax.broadcasted_iota(jnp.int32, (expert_count, tok), 0)
    named = jnp.zeros((expert_count, tok), f32)
    gate = jnp.zeros((expert_count, tok), f32)
    for k in range(route_ref.shape[0]):
        match = expert_row == route_ref[k:k + 1, :]
        named = named + jnp.where(match, 1.0, 0.0)
        gate = gate + jnp.where(match, gates_ref[k:k + 1, :], 0.0)
    before = jnp.where(
        lax.broadcasted_iota(jnp.int32, (tok, tok), 0) < lax.broadcasted_iota(jnp.int32, (tok, tok), 1),
        1.0, 0.0).astype(bf16)
    rank = dot(named.astype(bf16), before, ((1,), (0,)))
    tabs[z, j, :expert_count] = jnp.where(named > 0, rank, -1.0)
    tabs[z, j, expert_count:] = gate
    barrier = pltpu.get_barrier_semaphore()
    for d in range(1, sections):
        pl.semaphore_signal(barrier, inc=1, device_id=((z + d) % sections, j), device_id_type=MESH)
    for r in range(1, sources):
        pl.semaphore_signal(barrier, inc=1, device_id=(z, (j + r) % sources), device_id_type=MESH)
    pl.semaphore_wait(barrier, sections + sources - 2)

    own_dy = pltpu.make_async_copy(dy_ref, all_ref.at[z, pl.ds(pl.multiple_of(j * tok, tok), tok)], local_sem.at[0])
    get_w = pltpu.make_async_copy(w_ref, w_vm, local_sem.at[2])

    def remote(source, target, send, recv, to):
        return pltpu.make_async_remote_copy(
            source, target, send, recv, device_id=to, device_id_type=MESH)

    def block_at(s, block, start, count):
        return all_ref.at[s, pl.ds(pl.multiple_of(block * tok + start, 16), count)]

    z_copies, h_copies = [None], [None]
    for i in range(1, sections):
        to = (z + steps[i]) % sections
        z_copies.append([
            remote(dy_ref, block_at(z, j, 0, tok), z_send.at[i, 0], z_recv.at[i, 0], (to, j)),
            remote(tabs.at[z, j], tabs.at[z, j], z_send.at[i, 1], z_recv.at[i, 1], (to, j)),
        ])
        h_copies.append(remote(blocks_ref.at[to], parts.at[z], h_send.at[i], h_recv.at[i], (to, j)))

    stage = {}

    def begin(i, k):
        s = section_at(i)
        stage[i, k] = []
        for part in range(3):
            order = orders[part % 2]
            have = [[]]
            for bit in order[:k]:
                have = have + [r + [bit] for r in have]
            to = (z, flipped(j, [order[k]]))
            for r in have:
                block = flipped(j, r)
                slot = sum(r) + order[k]
                sems = e_send.at[i, part, slot], e_recv.at[i, part, slot]
                if part == 2:
                    copy = remote(tabs.at[s, block], tabs.at[s, block], *sems, to)
                else:
                    target = block_at(s, block, part * half_rows, half_rows)
                    source = target
                    if i == 0 and not r:
                        source = dy_ref.at[pl.ds(part * half_rows, half_rows)]
                    copy = remote(source, target, *sems, to)
                copy.start()
                stage[i, k].append(copy)

    def arrive(i, k):
        for copy in stage[i, k]:
            copy.wait_recv()

    last = len(bits) - 1

    def fetch(i):
        load = pltpu.make_async_copy(all_ref.at[section_at(i)], dy_vm, local_sem.at[3])
        load.start()
        load.wait()

    def row_of(i, p, row):
        s = section_at(i)
        return jnp.concatenate(
            [tabs[s, 2 * p, pl.ds(row, 1), :], tabs[s, 2 * p + 1, pl.ds(row, 1), :]], axis=1)

    def rank_row(i, p, e):
        rank = row_of(i, p, j * held + e)
        lane = lax.broadcasted_iota(jnp.int32, rank.shape, 1)
        return jnp.where(rank < 0, -1.0, rank + jnp.where(lane < tok, 0.0, float(capacity)))

    def gate_row(i, p, e):
        return row_of(i, p, expert_count + j * held + e)

    def chosen(i, p, e):
        place = lax.broadcasted_iota(jnp.int32, (pair_rows, 2 * tok), 0).astype(f32)
        return place == rank_row(i, p, e)

    def weight_part(i):
        s = section_at(i)
        for p in range(pairs):
            hid = parts[s, p * pair_rows:(p + 1) * pair_rows, :]
            for e in range(held):
                gates = jnp.where(chosen(i, p, e), gate_row(i, p, e), 0.0).astype(bf16)
                moved = dot(hid, gates, ((0,), (0,)))
                scattered[e * part_width:(e + 1) * part_width, p * 2 * tok:(p + 1) * 2 * tok] = (
                    moved[e * part_width:(e + 1) * part_width].astype(bf16))

        def tile(t, _):
            cols = pl.ds(pl.multiple_of(t * TILE, TILE), TILE)
            value = dot(scattered[...], dy_vm[:, cols], ((1,), (0,)))
            if i > 0:
                value = value + acc[:, cols]
            if i == sections - 1:
                dw_ref[:, cols] = value.astype(bf16)
            else:
                acc[:, cols] = value
            return 0

        lax.fori_loop(0, width // TILE, tile, 0)

    def hidden_part():
        for e in range(held):
            for p in range(pairs):
                picked[e, p] = jnp.where(chosen(0, p, e), 1.0, 0.0).astype(bf16)
            plain[e] = jnp.zeros(plain.shape[1:], f32)

        def tile(t, _):
            cols = pl.ds(pl.multiple_of(t * TILE, TILE), TILE)
            for e in range(held):
                for p in range(pairs):
                    rows_vm[p * pair_rows:(p + 1) * pair_rows, :] = dot(
                        picked[e, p], dy_vm[p * 2 * tok:(p + 1) * 2 * tok, cols], ((1,), (0,))
                    ).astype(bf16)
                plain[e] += dot(rows_vm[...], w_vm[e, :, cols], ((1,), (1,)))
            return 0

        lax.fori_loop(0, width // TILE, tile, 0)
        for e in range(held):
            for p in range(pairs):
                rows = slice(p * pair_rows, (p + 1) * pair_rows)
                here = chosen(0, p, e)
                gate = jnp.sum(jnp.where(here, gate_row(0, p, e), 0.0), axis=1, keepdims=True)
                value = plain[e, rows, :]
                dh_ref[e, rows, :] = (value * gate).astype(bf16)
                total = jnp.sum(value * hid_ref[e, rows, :].astype(f32), axis=1, keepdims=True)
                by_token = jnp.sum(jnp.where(here, total, 0.0), axis=0, keepdims=True)
                token_vm[2 * p, e:e + 1, :] = by_token[:, :tok]
                token_vm[2 * p + 1, e:e + 1, :] = by_token[:, tok:]

    b_copies = []
    for r in range(1, sources):
        to = (j + r) % sources
        b_copies.append(remote(token_vm.at[to], back_vm.at[j], b_send.at[r], b_recv.at[r], (z, to)))

    token_vm[...] = jnp.zeros(token_vm.shape, f32)
    begin(0, 0)
    own_dy.start()
    get_w.start()
    if sections > 1:
        for copy in z_copies[1]:
            copy.start()
    for s in range(sections):
        for e in range(held):
            blocks_ref[s, :, e * part_width:(e + 1) * part_width] = (
                hid_ref[e, :, s * part_width:(s + 1) * part_width])
    if sections > 1:
        h_copies[1].start()
    parts[z] = blocks_ref[z]
    for i in range(sections):
        for k in range(1, last):
            arrive(i, k - 1)
            begin(i, k)
        if i + 1 < sections:
            for copy in z_copies[i + 1]:
                copy.wait()
            begin(i + 1, 0)
            if i + 2 < sections:
                for copy in z_copies[i + 2]:
                    copy.start()
            if i >= 2:
                h_copies[i].start()
            if i + 2 == sections and i + 1 >= 2:
                h_copies[i + 1].start()
        if i == 1:
            get_w.wait()
            hidden_part()
            for copy in b_copies:
                copy.start()
            back_vm[j] = token_vm[j]
            weight_part(0)
        elif i >= 2:
            fetch(i - 1)
            h_copies[i - 1].wait_recv()
            weight_part(i - 1)
        arrive(i, last - 1)
        begin(i, last)
        if i == 0:
            own_dy.wait()
            arrive(0, last)
            fetch(0)
        elif i + 1 < sections:
            arrive(i, last)
    final = sections - 1
    arrive(final, last)
    fetch(final)
    h_copies[final].wait_recv()
    weight_part(final)
    for copy in b_copies:
        copy.wait()
    routed = jnp.zeros(route_ref.shape, f32)
    for e in range(expert_count):
        value = back_vm[e // held, e % held:e % held + 1, :]
        routed = routed + jnp.where(route_ref[...] == e, value, 0.0)
    dg_ref[...] = routed
    for copies in stage.values():
        for copy in copies:
            copy.wait_send()
    for copy in h_copies[1:]:
        copy.wait_send()


def fused(dy, routes, gates, hid, w, sections, sources):
    tok, width = dy.shape
    held, slot_rows, hidden_width = hid.shape
    part_rows = held * hidden_width // sections
    blocks = (sections, slot_rows, part_rows)
    pairs = sources // 2
    any_space, vmem = pl.BlockSpec(memory_space=pl.ANY), pl.BlockSpec(memory_space=pltpu.VMEM)
    dma = pltpu.SemaphoreType.DMA
    f32, bf16 = jnp.float32, jnp.bfloat16
    back = (sources, 8, tok)
    flops = 2 * width * (2 * slot_rows * held * hidden_width + sections * sources * tok * part_rows)
    return pl.pallas_call(
        functools.partial(body, sections, sources),
        out_shape=(
            jax.ShapeDtypeStruct((sections, sources * tok, width), bf16),
            jax.ShapeDtypeStruct((part_rows, width), bf16),
            jax.ShapeDtypeStruct(hid.shape, bf16),
            jax.ShapeDtypeStruct(routes.shape, f32),
        ),
        in_specs=[any_space, vmem, vmem, vmem, any_space],
        out_specs=(any_space, vmem, vmem, vmem),
        scratch_shapes=[
            pltpu.VMEM((sections, sources, 2 * held * sources, tok), f32),
            pltpu.VMEM(blocks, bf16),
            pltpu.VMEM(blocks, bf16),
            pltpu.VMEM((sources * tok, width), bf16),
            pltpu.VMEM(w.shape, bf16),
            pltpu.VMEM((part_rows, width), f32),
            pltpu.VMEM((part_rows, sources * tok), bf16),
            pltpu.VMEM((held, pairs, slot_rows // pairs, 2 * tok), bf16),
            pltpu.VMEM((slot_rows, TILE), bf16),
            pltpu.VMEM(hid.shape, f32),
            pltpu.VMEM(back, f32),
            pltpu.VMEM(back, f32),
            dma((4,)), dma((sections, 2)), dma((sections, 2)), dma((sections,)), dma((sections,)),
            dma((sections, 3, sources)), dma((sections, 3, sources)), dma((sources,)), dma((sources,)),
        ],
        compiler_params=pltpu.CompilerParams(
            collective_id=0, has_side_effects=True, vmem_limit_bytes=58 * 1024 * 1024),
        cost_estimate=pl.CostEstimate(
            flops=flops, bytes_accessed=2 * sections * sources * tok * width * 2, transcendentals=0),
    )(dy, routes, gates, hid, w)


def shards(d_output, gate_values, routes, hidden_saved, w_down):
    held, hidden_width, width = w_down.shape
    tok = d_output.shape[0]
    sources, capacity = hidden_saved.shape[2], hidden_saved.shape[3]
    sections = lax.axis_size("section")
    hid = hidden_saved.reshape(held, sources * capacity, hidden_width)
    _, d_weight, d_hidden, d_gate = fused(
        d_output, routes.T, gate_values.T.astype(jnp.float32), hid, w_down, sections, sources)
    return (
        d_hidden.reshape(hidden_saved.shape),
        d_weight.reshape(held, hidden_width // sections, width),
        d_gate.T,
    )


def solution(mesh):
    placed = (
        P(("section", "expert"), None),
        P(("section", "expert"), None),
        P(("section", "expert"), None),
        P("section", "expert", None, None, None),
        P("expert", None, None),
    )
    return jax.shard_map(
        shards,
        mesh=mesh,
        in_specs=placed,
        out_specs=(
            P("section", "expert", None, None, None),
            P("expert", "section", None),
            P(("section", "expert"), None),
        ),
        check_vma=False,
    )
```

```python
import functools

import jax
import jax.numpy as jnp
from jax import lax
from jax.experimental import pallas as pl
from jax.experimental.pallas import tpu as pltpu
from jax.sharding import PartitionSpec as P

MESH = pl.DeviceIdType.MESH
TILE = 512


def flipped(index, bits):
    for bit in bits:
        index = index + bit * (1 - 2 * ((index // bit) % 2))
    return index


def dot(a, b, dims):
    return lax.dot_general(a, b, (dims, ((), ())), preferred_element_type=jnp.float32)


def body(sections, sources, dy_ref, route_ref, gates_ref, hid_ref, w_ref,
         tok_ref, dw_ref, dh_ref, dg_ref,
         tabs, blocks_ref, parts, dy_vm, w_vm, acc, near, scattered, picked, rows_vm, plain,
         partner_rows, token_vm, back_vm,
         local_sem, fetch_sem, own_send, own_recv, z_send, z_recv, s_send, s_recv, h_send, h_recv,
         x_send, x_recv, o_send, o_recv, b_send, b_recv):
    f32, bf16 = jnp.float32, jnp.bfloat16
    z, j = lax.axis_index("section"), lax.axis_index("expert")
    tok, width = dy_ref.shape
    held, slot_rows, hidden_width = hid_ref.shape
    pairs = sources // 2
    pair_rows = slot_rows // pairs
    capacity = pair_rows // 2
    part_width = hidden_width // sections
    part_rows = held * part_width
    expert_count = held * sources
    half_rows = tok // 2
    chunks = tok_ref.shape[0]
    hops = sections - 1
    q = (j % 2) * pairs + j // 2
    bits = [1 << b for b in range(sources.bit_length() - 1)]
    orders = (bits, bits[:-1][::-1] + bits[-1:])
    half = q % 2

    def index_of(place):
        return (place % pairs) * 2 + place // pairs

    def device(place):
        return (z, index_of(place))

    def rows_at(place, start, count):
        return pl.ds(pl.multiple_of(place * tok + start, 16), count)

    def columns(k):
        return pl.ds(pl.multiple_of(half * (width // 2) + k * TILE, TILE), TILE)

    def remote(source, target, send, recv, to):
        return pltpu.make_async_remote_copy(
            source, target, send, recv, device_id=to, device_id_type=MESH)

    expert_row = lax.broadcasted_iota(jnp.int32, (expert_count, tok), 0)
    named = jnp.zeros((expert_count, tok), f32)
    gate = jnp.zeros((expert_count, tok), f32)
    for k in range(route_ref.shape[0]):
        match = expert_row == route_ref[k:k + 1, :]
        named = named + jnp.where(match, 1.0, 0.0)
        gate = gate + jnp.where(match, gates_ref[k:k + 1, :], 0.0)
    before = jnp.where(
        lax.broadcasted_iota(jnp.int32, (tok, tok), 0) < lax.broadcasted_iota(jnp.int32, (tok, tok), 1),
        1.0, 0.0).astype(bf16)
    rank = dot(named.astype(bf16), before, ((1,), (0,)))
    tabs[z, q, :expert_count] = jnp.where(named > 0, rank, -1.0)
    tabs[z, q, expert_count:] = gate

    barrier = pltpu.get_barrier_semaphore()
    for d in range(1, sections):
        pl.semaphore_signal(barrier, inc=1, device_id=((z + d) % sections, j), device_id_type=MESH)
    for r in range(1, sources):
        pl.semaphore_signal(barrier, inc=1, device_id=(z, (j + r) % sources), device_id_type=MESH)
    pl.semaphore_wait(barrier, sections + sources - 2)

    own_dy = pltpu.make_async_copy(dy_ref, dy_vm.at[rows_at(q, 0, tok)], local_sem.at[0])

    def get_w(e):
        return pltpu.make_async_copy(w_ref.at[e], w_vm, local_sem.at[1])


    own = []

    def begin(k):
        made = []
        for part in range(3):
            order = orders[part % 2]
            have = [[]]
            for bit in order[:k]:
                have = have + [r + [bit] for r in have]
            to = device(flipped(q, [order[k]]))
            for r in have:
                place = flipped(q, r)
                slot = sum(r) + order[k]
                sems = own_send.at[part, slot], own_recv.at[part, slot]
                if part == 2:
                    copy = remote(tabs.at[z, place], tabs.at[z, place], *sems, to)
                else:
                    target = dy_vm.at[rows_at(place, part * half_rows, half_rows)]
                    source = target if r else dy_ref.at[pl.ds(part * half_rows, half_rows)]
                    copy = remote(source, target, *sems, to)
                copy.start()
                made.append(copy)
        own.append(made)

    def arrive(k):
        for copy in own[k]:
            copy.wait_recv()

    def present(way, r):
        return z >= r + 1 if way == 0 else z + r + 1 < sections

    def z_valid(way, r):
        if way == 0:
            return jnp.logical_and(z >= r, z + 1 < sections)
        return jnp.logical_and(z + r < sections, z >= 1)

    def z_copies(k, way, r):
        s = (z - r + sections if way == 0 else z + r) % sections
        to = ((z + 1 if way == 0 else z - 1 + sections) % sections, j)
        low = q // 2 * 2
        target = tok_ref.at[k, s, rows_at(low, 0, 2 * tok)]
        source = dy_vm.at[rows_at(low, 0, 2 * tok), columns(k)] if r == 0 else target
        made = [remote(source, target, z_send.at[k, way, r], z_recv.at[k, way, r], to)]
        if k == 0:
            table = tabs.at[s, pl.ds(low, 2)]
            made.append(remote(
                table, table, z_send.at[chunks, way, r], z_recv.at[chunks, way, r], to))
        return made

    def plane_copies(k, way, r, b):
        s = (z - 1 - r + sections if way == 0 else z + 1 + r) % sections
        bit = bits[b]
        to = device(flipped(q, [bit]))
        low = q // bit * bit
        target = tok_ref.at[k, s, rows_at(low, 0, bit * tok)]
        made = [remote(target, target, s_send.at[k, way, r, b], s_recv.at[k, way, r, b], to)]
        if k == 0:
            table = tabs.at[s, pl.ds(low, bit)]
            made.append(remote(
                table, table, s_send.at[chunks, way, r, b], s_recv.at[chunks, way, r, b], to))
        return made

    def each_way(condition, r, work):
        for way in range(2):
            @pl.when(condition(way, r))
            def _():
                work(way)

    def start_all(copies):
        for copy in copies:
            copy.start()

    def wait_in(copies):
        for copy in copies:
            copy.wait_recv()

    def wait_out(copies):
        for copy in copies:
            copy.wait_send()

    h_copies, x_copies, fetches = [None], [], [None]
    mate = device(flipped(q, [1]))
    for i in range(sections):
        to = (z + i) % sections
        if i:
            h_copies.append(remote(
                blocks_ref.at[to], parts.at[0, z], h_send.at[i], h_recv.at[i], (to, j)))
        source = (z - i + sections) % sections
        x_copies.append(remote(
            parts.at[0, source], parts.at[1, source], x_send.at[i], x_recv.at[i], mate))

    def row_of(s, p, row):
        return jnp.concatenate(
            [tabs[s, p, pl.ds(row, 1), :], tabs[s, pairs + p, pl.ds(row, 1), :]], axis=1)

    def gate_row(s, p, expert):
        return row_of(s, p, expert_count + expert)

    def chosen(s, p, expert):
        rank = row_of(s, p, expert)
        lane = lax.broadcasted_iota(jnp.int32, rank.shape, 1)
        rank = jnp.where(rank < 0, -1.0, rank + jnp.where(lane < tok, 0.0, float(capacity)))
        place = lax.broadcasted_iota(jnp.int32, (pair_rows, 2 * tok), 0).astype(f32)
        return place == rank

    def scatter_part():
        mate_index = index_of(flipped(q, [1]))

        def one(i, _):
            s = (z + i) % sections
            for o, first in ((0, j * held), (1, mate_index * held)):
                for p in range(pairs):
                    hid = parts[o, s, p * pair_rows:(p + 1) * pair_rows, :]
                    for e in range(held):
                        gates = jnp.where(
                            chosen(s, p, first + e), gate_row(s, p, first + e), 0.0).astype(bf16)
                        rows = slice(e * part_width, (e + 1) * part_width)
                        moved = dot(hid, gates, ((0,), (0,)))[rows].astype(bf16)
                        at = o * part_rows + e * part_width
                        for c in range(2):
                            start = pl.multiple_of(i * (sources * tok) + (c * pairs + p) * tok, tok)
                            scattered[at:at + part_width, pl.ds(start, tok)] = (
                                moved[:, c * tok:(c + 1) * tok])
            return 0

        lax.fori_loop(0, sections, one, 0)

    o_copies = []

    def weight_chunk(k):
        def fetch(i):
            return pltpu.make_async_copy(
                tok_ref.at[k, (z + i) % sections], near.at[i % 2], fetch_sem.at[i % 2])

        if sections > 1:
            fetch(1).start()
        acc[...] = dot(scattered[:, :sources * tok], dy_vm[:, columns(k)], ((1,), (0,)))

        def one(i, _):
            fetch(i).wait()

            @pl.when(i + 1 < sections)
            def _():
                fetch(i + 1).start()

            start = pl.multiple_of(i * (sources * tok), tok)
            acc[...] += dot(
                scattered[:, pl.ds(start, sources * tok)], near[i % 2], ((1,), (0,)))
            return 0

        lax.fori_loop(1, sections, one, 0)
        partner_rows[k] = acc[part_rows:].astype(bf16)
        copy = remote(
            partner_rows.at[k], dw_ref.at[:, columns(k)], o_send.at[k], o_recv.at[k], mate)
        copy.start()
        o_copies.append(copy)
        dw_ref[:, columns(k)] = acc[:part_rows].astype(bf16)

    b_copies = []
    for r in range(1, sources):
        to = (j + r) % sources
        b_copies.append(remote(token_vm.at[to], back_vm.at[j], b_send.at[r], b_recv.at[r], (z, to)))

    def hidden_tiles(e, first, count):
        def tile(t, _):
            cols = pl.ds(pl.multiple_of(t * TILE, TILE), TILE)
            for p in range(pairs):
                tokens = jnp.concatenate(
                    [dy_vm[p * tok:(p + 1) * tok, cols],
                     dy_vm[(pairs + p) * tok:(pairs + p + 1) * tok, cols]], axis=0)
                rows_vm[p * pair_rows:(p + 1) * pair_rows, :] = dot(
                    picked[e, p], tokens, ((1,), (0,))).astype(bf16)
            plain[...] += dot(rows_vm[...], w_vm[:, cols], ((1,), (1,)))
            return 0

        lax.fori_loop(first, first + count, tile, 0)

    def hidden_start():
        for e in range(held):
            for p in range(pairs):
                picked[e, p] = jnp.where(chosen(z, p, j * held + e), 1.0, 0.0).astype(bf16)

    def hidden_next(e):
        if e:
            get_w(e).start()
        plain[...] = jnp.zeros(plain.shape, f32)
        get_w(e).wait()

    def hidden_done(e):
        for p in range(pairs):
            rows = slice(p * pair_rows, (p + 1) * pair_rows)
            here = chosen(z, p, j * held + e)
            gate = jnp.sum(
                jnp.where(here, gate_row(z, p, j * held + e), 0.0), axis=1, keepdims=True)
            value = plain[rows, :]
            dh_ref[e, rows, :] = (value * gate).astype(bf16)
            total = jnp.sum(value * hid_ref[e, rows, :].astype(f32), axis=1, keepdims=True)
            by_token = jnp.sum(jnp.where(here, total, 0.0), axis=0, keepdims=True)
            token_vm[2 * p, e:e + 1, :] = by_token[:, :tok]
            token_vm[2 * p + 1, e:e + 1, :] = by_token[:, tok:]

    def hidden_end():
        for copy in b_copies:
            copy.start()
        back_vm[j] = token_vm[j]

    tiles = width // TILE
    step = max(1, tiles // 4)
    work = [hidden_start]
    for e in range(held):
        work.append(functools.partial(hidden_next, e))
        for first in range(0, tiles, step):
            work.append(functools.partial(hidden_tiles, e, first, min(step, tiles - first)))
        work.append(functools.partial(hidden_done, e))
    work.append(hidden_end)

    def some(count):
        for _ in range(count):
            if work:
                work.pop(0)()

    last = len(bits) - 1
    begin(0)
    own_dy.start()
    get_w(0).start()
    for s in range(sections):
        for e in range(held):
            blocks_ref[s, :, e * part_width:(e + 1) * part_width] = (
                hid_ref[e, :, s * part_width:(s + 1) * part_width])
    start_all(h_copies[1:])
    parts[0, z] = blocks_ref[z]
    token_vm[...] = jnp.zeros(token_vm.shape, f32)
    for k in range(1, last):
        arrive(k - 1)
        begin(k)
    x_copies[0].start()
    own_dy.wait()
    arrive(last - 1)
    for k in range(chunks):
        each_way(z_valid, 0, lambda way: start_all(z_copies(k, way, 0)))
    begin(last)
    for i in range(1, sections):
        h_copies[i].wait_recv()
        x_copies[i].start()
    arrive(last)
    some(1)
    units = [(k, r) for k in range(chunks) for r in range(hops)]
    built = False
    for t in range(len(units) + last):
        if t < len(units):
            k, r = units[t]

            def forward(way):
                wait_in(z_copies(k, way, r))
                start_all(plane_copies(k, way, r, 1))

            each_way(present, r, forward)
            if r + 1 < hops:
                each_way(z_valid, r + 1, lambda way: start_all(z_copies(k, way, r + 1)))
        for b in range(1, last + 1):
            if 0 <= t - b < len(units):
                k, r = units[t - b]

                def pass_on(way):
                    wait_in(plane_copies(k, way, r, b))
                    if b < last:
                        start_all(plane_copies(k, way, r, b + 1))

                each_way(present, r, pass_on)
        some(2)
        if t >= last and (t - last + 1) % hops == 0:
            if not built:
                for copy in x_copies:
                    copy.wait_recv()
                scatter_part()
                built = True
            weight_chunk((t - last) // hops)
    some(len(work))
    for copy in b_copies:
        copy.wait()
    routed = jnp.zeros(route_ref.shape, f32)
    for e in range(expert_count):
        value = back_vm[e // held, e % held:e % held + 1, :]
        routed = routed + jnp.where(route_ref[...] == e, value, 0.0)
    dg_ref[...] = routed
    for copies in own:
        wait_out(copies)
    wait_out(h_copies[1:])
    wait_out(x_copies)
    for k, r in units:
        each_way(z_valid, r, lambda way: wait_out(z_copies(k, way, r)))
        for b in range(1, last + 1):
            each_way(present, r, lambda way: wait_out(plane_copies(k, way, r, b)))
    for copy in o_copies:
        copy.wait()


def fused(dy, routes, gates, hid, w, sections, sources):
    tok, width = dy.shape
    held, slot_rows, hidden_width = hid.shape
    part_rows = held * hidden_width // sections
    blocks = (sections, slot_rows, part_rows)
    pairs = sources // 2
    chunks = width // 2 // TILE
    stages = sources.bit_length() - 1
    any_space, vmem = pl.BlockSpec(memory_space=pl.ANY), pl.BlockSpec(memory_space=pltpu.VMEM)
    dma = pltpu.SemaphoreType.DMA
    f32, bf16 = jnp.float32, jnp.bfloat16
    back = (sources, 8, tok)
    flops = 2 * width * (2 * slot_rows * held * hidden_width + sections * sources * tok * part_rows)
    hops = max(1, sections - 1)
    return pl.pallas_call(
        functools.partial(body, sections, sources),
        out_shape=(
            jax.ShapeDtypeStruct((chunks, sections, sources * tok, TILE), bf16),
            jax.ShapeDtypeStruct((part_rows, width), bf16),
            jax.ShapeDtypeStruct(hid.shape, bf16),
            jax.ShapeDtypeStruct(routes.shape, f32),
        ),
        in_specs=[any_space, vmem, vmem, vmem, any_space],
        out_specs=(any_space, vmem, vmem, vmem),
        scratch_shapes=[
            pltpu.VMEM((sections, sources, 2 * held * sources, tok), f32),
            pltpu.VMEM(blocks, bf16),
            pltpu.VMEM((2,) + blocks, bf16),
            pltpu.VMEM((sources * tok, width), bf16),
            pltpu.VMEM(w.shape[1:], bf16),
            pltpu.VMEM((2 * part_rows, TILE), f32),
            pltpu.VMEM((2, sources * tok, TILE), bf16),
            pltpu.VMEM((2 * part_rows, sections * sources * tok), bf16),
            pltpu.VMEM((held, pairs, slot_rows // pairs, 2 * tok), bf16),
            pltpu.VMEM((slot_rows, TILE), bf16),
            pltpu.VMEM(hid.shape[1:], f32),
            pltpu.VMEM((chunks, part_rows, TILE), bf16),
            pltpu.VMEM(back, f32),
            pltpu.VMEM(back, f32),
            dma((2,)), dma((2,)), dma((3, sources)), dma((3, sources)),
            dma((chunks + 1, 2, hops)), dma((chunks + 1, 2, hops)),
            dma((chunks + 1, 2, hops, stages)), dma((chunks + 1, 2, hops, stages)),
            dma((sections,)), dma((sections,)), dma((sections,)), dma((sections,)),
            dma((chunks,)), dma((chunks,)), dma((sources,)), dma((sources,)),
        ],
        compiler_params=pltpu.CompilerParams(
            collective_id=0, has_side_effects=True, vmem_limit_bytes=60 * 1024 * 1024),
        cost_estimate=pl.CostEstimate(
            flops=flops, bytes_accessed=sections * sources * tok * width * 2, transcendentals=0),
    )(dy, routes, gates, hid, w)


def shards(d_output, gate_values, routes, hidden_saved, w_down):
    held, hidden_width, width = w_down.shape
    tok = d_output.shape[0]
    sources, capacity = hidden_saved.shape[2], hidden_saved.shape[3]
    sections = lax.axis_size("section")
    hid = hidden_saved.reshape(held, sources * capacity, hidden_width)
    _, d_weight, d_hidden, d_gate = fused(
        d_output, routes.T, gate_values.T.astype(jnp.float32), hid, w_down, sections, sources)
    return (
        d_hidden.reshape(hidden_saved.shape),
        d_weight.reshape(held, hidden_width // sections, width),
        d_gate.T,
    )


def solution(mesh):
    placed = (
        P(("section", "expert"), None),
        P(("section", "expert"), None),
        P(("section", "expert"), None),
        P("section", "expert", None, None, None),
        P("expert", None, None),
    )
    return jax.shard_map(
        shards,
        mesh=mesh,
        in_specs=placed,
        out_specs=(
            P("section", "expert", None, None, None),
            P("expert", "section", None),
            P(("section", "expert"), None),
        ),
        check_vma=False,
    )
```

```python
import functools

import jax
import jax.numpy as jnp
from jax import lax
from jax.experimental import pallas as pl
from jax.experimental.pallas import tpu as pltpu
from jax.sharding import PartitionSpec as P

MESH = pl.DeviceIdType.MESH
TILE = 512


def chunk_spans(width):
    half = width // 2
    spans = [(at, TILE) for at in range(0, half - TILE, TILE)]
    return spans + [(half - TILE, TILE // 2), (half - TILE // 2, TILE // 2)]


def flipped(index, bits):
    for bit in bits:
        index = index + bit * (1 - 2 * ((index // bit) % 2))
    return index


def dot(a, b, dims):
    return lax.dot_general(a, b, (dims, ((), ())), preferred_element_type=jnp.float32)


def body(sections, sources, dy_ref, route_ref, gates_ref, hid_ref, w_ref,
         tok_ref, dw_ref, dh_ref, dg_ref,
         tabs, blocks_ref, parts, dy_vm, w_vm, acc, near, scattered, picked, rows_vm, plain,
         partner_rows, token_vm, back_vm,
         local_sem, fetch_sem, own_send, own_recv, z_send, z_recv, s_send, s_recv, h_send, h_recv,
         x_send, x_recv, o_send, o_recv, b_send, b_recv):
    f32, bf16 = jnp.float32, jnp.bfloat16
    z, j = lax.axis_index("section"), lax.axis_index("expert")
    tok, width = dy_ref.shape
    held, slot_rows, hidden_width = hid_ref.shape
    pairs = sources // 2
    pair_rows = slot_rows // pairs
    capacity = pair_rows // 2
    part_width = hidden_width // sections
    part_rows = held * part_width
    expert_count = held * sources
    half_rows = tok // 2
    spans = chunk_spans(width)
    chunks = len(spans)
    hops = sections - 1
    q = (j % 2) * pairs + j // 2
    bits = [1 << b for b in range(sources.bit_length() - 1)]
    orders = (bits, bits[:-1][::-1] + bits[-1:])
    half = q % 2

    def index_of(place):
        return (place % pairs) * 2 + place // pairs

    def device(place):
        return (z, index_of(place))

    def rows_at(place, start, count):
        return pl.ds(pl.multiple_of(place * tok + start, 16), count)

    def columns(k):
        at, size = spans[k]
        return pl.ds(pl.multiple_of(half * (width // 2) + at, TILE // 2), size)

    def local_columns(k):
        return pl.ds(*spans[k])

    def remote(source, target, send, recv, to):
        return pltpu.make_async_remote_copy(
            source, target, send, recv, device_id=to, device_id_type=MESH)

    barrier = pltpu.get_barrier_semaphore()
    for d in range(1, sections):
        pl.semaphore_signal(barrier, inc=1, device_id=((z + d) % sections, j), device_id_type=MESH)
    for r in range(1, sources):
        pl.semaphore_signal(barrier, inc=1, device_id=(z, (j + r) % sources), device_id_type=MESH)
    expert_row = lax.broadcasted_iota(jnp.int32, (expert_count, tok), 0)
    named = jnp.zeros((expert_count, tok), f32)
    gate = jnp.zeros((expert_count, tok), f32)
    for k in range(route_ref.shape[0]):
        match = expert_row == route_ref[k:k + 1, :]
        named = named + jnp.where(match, 1.0, 0.0)
        gate = gate + jnp.where(match, gates_ref[k:k + 1, :], 0.0)
    before = jnp.where(
        lax.broadcasted_iota(jnp.int32, (tok, tok), 0) < lax.broadcasted_iota(jnp.int32, (tok, tok), 1),
        1.0, 0.0).astype(bf16)
    rank = dot(named.astype(bf16), before, ((1,), (0,)))
    tabs[z, q, :expert_count] = jnp.where(named > 0, rank, -1.0)
    tabs[z, q, expert_count:] = gate

    pl.semaphore_wait(barrier, sections + sources - 2)

    own_dy = pltpu.make_async_copy(dy_ref, dy_vm.at[rows_at(q, 0, tok)], local_sem.at[0])

    def get_w(e):
        return pltpu.make_async_copy(w_ref.at[e], w_vm, local_sem.at[1])


    own = []

    def begin(k):
        made = []
        for part in range(3):
            order = orders[part % 2]
            have = [[]]
            for bit in order[:k]:
                have = have + [r + [bit] for r in have]
            to = device(flipped(q, [order[k]]))
            for r in have:
                place = flipped(q, r)
                slot = sum(r) + order[k]
                sems = own_send.at[part, slot], own_recv.at[part, slot]
                if part == 2:
                    copy = remote(tabs.at[z, place], tabs.at[z, place], *sems, to)
                else:
                    target = dy_vm.at[rows_at(place, part * half_rows, half_rows)]
                    source = target if r else dy_ref.at[pl.ds(part * half_rows, half_rows)]
                    copy = remote(source, target, *sems, to)
                copy.start()
                made.append(copy)
        own.append(made)

    def arrive(k):
        for copy in own[k]:
            copy.wait_recv()

    def present(way, r):
        return z >= r + 1 if way == 0 else z + r + 1 < sections

    def z_valid(way, r):
        if way == 0:
            return jnp.logical_and(z >= r, z + 1 < sections)
        return jnp.logical_and(z + r < sections, z >= 1)

    def z_copies(k, way, r):
        s = (z - r + sections if way == 0 else z + r) % sections
        to = ((z + 1 if way == 0 else z - 1 + sections) % sections, j)
        low = q // 2 * 2
        target = tok_ref.at[s, rows_at(low, 0, 2 * tok), local_columns(k)]
        source = dy_vm.at[rows_at(low, 0, 2 * tok), columns(k)] if r == 0 else target
        made = [remote(source, target, z_send.at[k, way, r], z_recv.at[k, way, r], to)]
        if k == 0:
            table = tabs.at[s, pl.ds(low, 2)]
            made.append(remote(
                table, table, z_send.at[chunks, way, r], z_recv.at[chunks, way, r], to))
        return made

    def plane_copies(k, way, r, b):
        s = (z - 1 - r + sections if way == 0 else z + 1 + r) % sections
        bit = bits[b]
        to = device(flipped(q, [bit]))
        low = q // bit * bit
        target = tok_ref.at[s, rows_at(low, 0, bit * tok), local_columns(k)]
        made = [remote(target, target, s_send.at[k, way, r, b], s_recv.at[k, way, r, b], to)]
        if k == 0:
            table = tabs.at[s, pl.ds(low, bit)]
            made.append(remote(
                table, table, s_send.at[chunks, way, r, b], s_recv.at[chunks, way, r, b], to))
        return made

    def each_way(condition, r, work):
        for way in range(2):
            @pl.when(condition(way, r))
            def _():
                work(way)

    def start_all(copies):
        for copy in copies:
            copy.start()

    def wait_in(copies):
        for copy in copies:
            copy.wait_recv()

    def wait_out(copies):
        for copy in copies:
            copy.wait_send()

    h_copies, x_copies, fetches = [None], [], [None]
    mate = device(flipped(q, [1]))
    for i in range(sections):
        to = (z + i) % sections
        if i:
            h_copies.append(remote(
                blocks_ref.at[to], parts.at[0, z], h_send.at[i], h_recv.at[i], (to, j)))
        source = (z - i + sections) % sections
        x_copies.append(remote(
            parts.at[0, source], parts.at[1, source], x_send.at[i], x_recv.at[i], mate))

    def row_of(s, p, row):
        return jnp.concatenate(
            [tabs[s, p, pl.ds(row, 1), :], tabs[s, pairs + p, pl.ds(row, 1), :]], axis=1)

    def gate_row(s, p, expert):
        return row_of(s, p, expert_count + expert)

    def chosen(s, p, expert, before=0, count=pair_rows):
        rank = row_of(s, p, expert)
        lane = lax.broadcasted_iota(jnp.int32, rank.shape, 1)
        rank = jnp.where(rank < 0, -1.0, rank + jnp.where(lane < tok, 0.0, float(capacity)))
        place = lax.broadcasted_iota(jnp.int32, (count, 2 * tok), 0).astype(f32)
        return place == jnp.where(rank < 0, -1.0, rank + float(before))

    def scatter_part():
        mate_index = index_of(flipped(q, [1]))

        def one(i, _):
            s = (z + i) % sections
            for o, first in ((0, j * held), (1, mate_index * held)):
                for p in range(pairs):
                    low = p * pair_rows // 128 * 128
                    high = -(-(p + 1) * pair_rows // 128) * 128
                    for e in range(held):
                        here = chosen(s, p, first + e, p * pair_rows - low, high - low)
                        gates = jnp.where(here, gate_row(s, p, first + e), 0.0).astype(bf16)
                        at = o * part_rows + e * part_width
                        rows = slice(e * part_width, (e + 1) * part_width)
                        moved = dot(
                            parts[o, s, rows, low:high], gates, ((1,), (0,))).astype(bf16)
                        for c in range(2):
                            start = pl.multiple_of(i * (sources * tok) + (c * pairs + p) * tok, tok)
                            scattered[at:at + part_width, pl.ds(start, tok)] = (
                                moved[:, c * tok:(c + 1) * tok])
            return 0

        lax.fori_loop(0, sections, one, 0)

    o_copies = []

    def fetch(k, i):
        size = spans[k][1]
        return pltpu.make_async_copy(
            tok_ref.at[(z + i) % sections, :, local_columns(k)],
            near.at[i % 2, :, pl.ds(0, size)], fetch_sem.at[i % 2])

    def add_section(k, i):
        size = spans[k][1]
        start = i * (sources * tok)
        if not isinstance(i, int):
            start = pl.multiple_of(start, tok)
        acc[:, :size] += dot(
            scattered[:, pl.ds(start, sources * tok)], near[i % 2, :, :size], ((1,), (0,)))

    def weight_own(k):
        acc[:, :spans[k][1]] = dot(
            scattered[:, :sources * tok], dy_vm[:, columns(k)], ((1,), (0,)))

    def weight_late(k, way, r):
        i = sections - 1 - r if way == 0 else 1 + r
        fetch(k, i).start()
        fetch(k, i).wait()
        add_section(k, i)

    def weight_rest(k):
        fetch(k, 1).start()
        weight_own(k)

        def one(i, _):
            fetch(k, i).wait()

            @pl.when(i + 1 < sections)
            def _():
                fetch(k, i + 1).start()

            add_section(k, i)
            return 0

        lax.fori_loop(1, sections, one, 0)

    def weight_out(k):
        size = spans[k][1]
        partner_rows[:, local_columns(k)] = acc[part_rows:, :size].astype(bf16)
        copy = remote(
            partner_rows.at[:, local_columns(k)], dw_ref.at[:, columns(k)],
            o_send.at[k], o_recv.at[k], mate)
        copy.start()
        o_copies.append(copy)
        dw_ref[:, columns(k)] = acc[:part_rows, :size].astype(bf16)

    b_copies = []
    for r in range(1, sources):
        to = (j + r) % sources
        b_copies.append(remote(token_vm.at[to], back_vm.at[j], b_send.at[r], b_recv.at[r], (z, to)))

    def hidden_tiles(e, first, count):
        def tile(t, _):
            cols = pl.ds(pl.multiple_of(t * TILE, TILE), TILE)
            for p in range(pairs):
                tokens = jnp.concatenate(
                    [dy_vm[p * tok:(p + 1) * tok, cols],
                     dy_vm[(pairs + p) * tok:(pairs + p + 1) * tok, cols]], axis=0)
                rows_vm[p * pair_rows:(p + 1) * pair_rows, :] = dot(
                    picked[e, p], tokens, ((1,), (0,))).astype(bf16)
            plain[...] += dot(rows_vm[...], w_vm[:, cols], ((1,), (1,)))
            return 0

        lax.fori_loop(first, first + count, tile, 0)

    def hidden_start():
        for e in range(held):
            for p in range(pairs):
                picked[e, p] = jnp.where(chosen(z, p, j * held + e), 1.0, 0.0).astype(bf16)

    def hidden_next(e):
        if e:
            get_w(e).start()
        plain[...] = jnp.zeros(plain.shape, f32)
        get_w(e).wait()

    def hidden_done(e):
        for p in range(pairs):
            rows = slice(p * pair_rows, (p + 1) * pair_rows)
            here = chosen(z, p, j * held + e)
            gate = jnp.sum(
                jnp.where(here, gate_row(z, p, j * held + e), 0.0), axis=1, keepdims=True)
            value = plain[rows, :]
            dh_ref[e, rows, :] = (value * gate).astype(bf16)
            total = jnp.sum(value * hid_ref[e, rows, :].astype(f32), axis=1, keepdims=True)
            by_token = jnp.sum(jnp.where(here, total, 0.0), axis=0, keepdims=True)
            token_vm[2 * p, e:e + 1, :] = by_token[:, :tok]
            token_vm[2 * p + 1, e:e + 1, :] = by_token[:, tok:]

    def hidden_end():
        for copy in b_copies:
            copy.start()
        back_vm[j] = token_vm[j]

    tiles = width // TILE
    step = max(1, tiles // 4)
    work = [hidden_start]
    for e in range(held):
        work.append(functools.partial(hidden_next, e))
        for first in range(0, tiles, step):
            work.append(functools.partial(hidden_tiles, e, first, min(step, tiles - first)))
        work.append(functools.partial(hidden_done, e))
    work.append(hidden_end)

    def some(count):
        for _ in range(count):
            if work:
                work.pop(0)()

    last = len(bits) - 1
    begin(0)
    own_dy.start()
    get_w(0).start()
    if blocks_ref.shape[2] > slot_rows:
        blocks_ref[...] = jnp.zeros(blocks_ref.shape, bf16)
    for s in range(sections):
        for e in range(held):
            blocks_ref[s, e * part_width:(e + 1) * part_width, :slot_rows] = jnp.transpose(
                hid_ref[e, :, s * part_width:(s + 1) * part_width])
    start_all(h_copies[1:])
    parts[0, z] = blocks_ref[z]
    token_vm[...] = jnp.zeros(token_vm.shape, f32)
    for k in range(1, last):
        arrive(k - 1)
        begin(k)
    x_copies[0].start()
    own_dy.wait()
    arrive(last - 1)
    for k in range(chunks):
        each_way(z_valid, 0, lambda way: start_all(z_copies(k, way, 0)))
    begin(last)
    for i in range(1, sections):
        h_copies[i].wait_recv()
        x_copies[i].start()
    arrive(last)
    some(1)
    units = [(k, r) for k in range(chunks) for r in range(hops)]
    built = False
    for t in range(len(units) + last):
        if t < len(units):
            k, r = units[t]

            def forward(way):
                wait_in(z_copies(k, way, r))
                start_all(plane_copies(k, way, r, 1))

            each_way(present, r, forward)
            if r + 1 < hops:
                each_way(z_valid, r + 1, lambda way: start_all(z_copies(k, way, r + 1)))
        for b in range(1, last + 1):
            if 0 <= t - b < len(units):
                k, r = units[t - b]

                def pass_on(way):
                    wait_in(plane_copies(k, way, r, b))
                    if b < last:
                        start_all(plane_copies(k, way, r, b + 1))

                each_way(present, r, pass_on)
        some(2)
        if t < last:
            continue
        k, r = units[t - last]
        if not built and r == hops - 1:
            for copy in x_copies:
                copy.wait_recv()
            scatter_part()
            built = True
        if k < chunks - 1:
            if r == hops - 1:
                weight_rest(k)
                weight_out(k)
                if k == chunks - 2:
                    weight_own(k + 1)
        else:
            each_way(present, r, lambda way: weight_late(k, way, r))
            if r == hops - 1:
                weight_out(k)
    some(len(work))
    for copy in b_copies:
        copy.wait()
    routed = jnp.zeros(route_ref.shape, f32)
    for e in range(expert_count):
        value = back_vm[e // held, e % held:e % held + 1, :]
        routed = routed + jnp.where(route_ref[...] == e, value, 0.0)
    dg_ref[...] = routed
    for copies in own:
        wait_out(copies)
    wait_out(h_copies[1:])
    wait_out(x_copies)
    for k, r in units:
        each_way(z_valid, r, lambda way: wait_out(z_copies(k, way, r)))
        for b in range(1, last + 1):
            each_way(present, r, lambda way: wait_out(plane_copies(k, way, r, b)))
    for copy in o_copies:
        copy.wait()


def fused(dy, routes, gates, hid, w, sections, sources):
    tok, width = dy.shape
    held, slot_rows, hidden_width = hid.shape
    part_rows = held * hidden_width // sections
    blocks = (sections, part_rows, -(-slot_rows // 128) * 128)
    pairs = sources // 2
    chunks = len(chunk_spans(width))
    stages = sources.bit_length() - 1
    any_space, vmem = pl.BlockSpec(memory_space=pl.ANY), pl.BlockSpec(memory_space=pltpu.VMEM)
    dma = pltpu.SemaphoreType.DMA
    f32, bf16 = jnp.float32, jnp.bfloat16
    back = (sources, 8, tok)
    flops = 2 * width * (2 * slot_rows * held * hidden_width + sections * sources * tok * part_rows)
    hops = max(1, sections - 1)
    return pl.pallas_call(
        functools.partial(body, sections, sources),
        out_shape=(
            jax.ShapeDtypeStruct((sections, sources * tok, width // 2), bf16),
            jax.ShapeDtypeStruct((part_rows, width), bf16),
            jax.ShapeDtypeStruct(hid.shape, bf16),
            jax.ShapeDtypeStruct(routes.shape, f32),
        ),
        in_specs=[any_space, vmem, vmem, vmem, any_space],
        out_specs=(any_space, vmem, vmem, vmem),
        scratch_shapes=[
            pltpu.VMEM((sections, sources, 2 * held * sources, tok), f32),
            pltpu.VMEM(blocks, bf16),
            pltpu.VMEM((2,) + blocks, bf16),
            pltpu.VMEM((sources * tok, width), bf16),
            pltpu.VMEM(w.shape[1:], bf16),
            pltpu.VMEM((2 * part_rows, TILE), f32),
            pltpu.VMEM((2, sources * tok, TILE), bf16),
            pltpu.VMEM((2 * part_rows, sections * sources * tok), bf16),
            pltpu.VMEM((held, pairs, slot_rows // pairs, 2 * tok), bf16),
            pltpu.VMEM((slot_rows, TILE), bf16),
            pltpu.VMEM(hid.shape[1:], f32),
            pltpu.VMEM((part_rows, width // 2), bf16),
            pltpu.VMEM(back, f32),
            pltpu.VMEM(back, f32),
            dma((2,)), dma((2,)), dma((3, sources)), dma((3, sources)),
            dma((chunks + 1, 2, hops)), dma((chunks + 1, 2, hops)),
            dma((chunks + 1, 2, hops, stages)), dma((chunks + 1, 2, hops, stages)),
            dma((sections,)), dma((sections,)), dma((sections,)), dma((sections,)),
            dma((chunks,)), dma((chunks,)), dma((sources,)), dma((sources,)),
        ],
        compiler_params=pltpu.CompilerParams(
            collective_id=0, has_side_effects=True, vmem_limit_bytes=60 * 1024 * 1024),
        cost_estimate=pl.CostEstimate(
            flops=flops, bytes_accessed=sections * sources * tok * width * 2, transcendentals=0),
    )(dy, routes, gates, hid, w)


def shards(d_output, gate_values, routes, hidden_saved, w_down):
    held, hidden_width, width = w_down.shape
    tok = d_output.shape[0]
    sources, capacity = hidden_saved.shape[2], hidden_saved.shape[3]
    sections = lax.axis_size("section")
    hid = hidden_saved.reshape(held, sources * capacity, hidden_width)
    _, d_weight, d_hidden, d_gate = fused(
        d_output, routes.T, gate_values.T.astype(jnp.float32), hid, w_down, sections, sources)
    return (
        d_hidden.reshape(hidden_saved.shape),
        d_weight.reshape(held, hidden_width // sections, width),
        d_gate.T,
    )


def solution(mesh):
    placed = (
        P(("section", "expert"), None),
        P(("section", "expert"), None),
        P(("section", "expert"), None),
        P("section", "expert", None, None, None),
        P("expert", None, None),
    )
    return jax.shard_map(
        shards,
        mesh=mesh,
        in_specs=placed,
        out_specs=(
            P("section", "expert", None, None, None),
            P("expert", "section", None),
            P(("section", "expert"), None),
        ),
        check_vma=False,
    )
```
